512 devices in a mesh: seq: 16 (over x, y_hi, core), chan: 16 (over z), batch: 2 (over y_lo).
Axes of the slice: x: 4, y: 4 (y_hi: 2, y_lo: 2; y = y_hi * 2 + y_lo), z: 16, core: 2. Of those that a mesh axis runs over, the one named last changes fastest.
Arguments:
- tokens: bfloat16 [8192, 4096], P(('batch', 'seq'), 'chan'), parts along dimension 0, may hold values from -6 to 6
- in_weights: bfloat16 [3, 4096, 4096], P(None, 'seq', 'chan'), may hold values from -0.09375 to 0.09375
- out_weights: bfloat16 [4096, 4096], P('seq', 'chan'), may hold values from -0.09375 to 0.09375
- spectrum: float32 [2, 4096, 8192], P(None, 'chan', 'seq'), may hold values from -6 to 6
Outputs:
- output: bfloat16 [8192, 4096], P(('batch', 'seq'), 'chan'), parts along dimension 0
The draws below stay inside these ranges and needn't reach their ends.
There are 2 independent parts, one for each index of `batch`. The reference program is written for one: setup_inputs(seed, part) draws one part's arguments, and reference() takes and returns one part's arrays. A program takes and returns all parts, laid end to end along the dimension named above; an argument that names none is the same for every part. Nothing has to cross between parts.
All inputs are finite; a program needn't handle non-finite values.
Results may differ from the reference program's by a relative error of at most 0.014.
Values may be sent and summed in bfloat16 or wider, within the bound.
A program may use at most 64 MiB of HBM per device.

```python
import jax
import jax.numpy as jnp

D = 4096
LENGTH = 4096
FFT_LEN = 8192


def levels(key, extent, cuts, smallest, largest):
    gain = 1.0
    for axis_at, parts in cuts:
        draws = jax.random.uniform(jax.random.fold_in(jax.random.fold_in(key, 6), axis_at), (parts,), jnp.float32, smallest / len(cuts), largest / len(cuts))
        gain = gain * jnp.repeat(jnp.exp(draws), extent[axis_at] // parts).reshape((-1,) + (1,) * (len(extent) - 1 - axis_at))
    return gain


def centred(stream_key, shape, width, limit, split=(), kind=jnp.bfloat16):
    array = jax.random.normal(stream_key, shape, jnp.float32) * width
    if len(split) > 0:
        array = levels(stream_key, shape, split, -0.22, 0.18) * array
    return jnp.clip(array, min=-limit, max=limit).astype(kind)


def setup_inputs(seed: int = 0, part: int = 0) -> dict:
    splits = jax.random.split(jax.random.key(seed), 5)
    part_keys = jax.random.split(jax.random.fold_in(splits[4], part), 5)
    return {
        "tokens": centred(part_keys[0], (LENGTH, D), 1.0, 6.0, ((0, 16), (1, 16))),
        "in_weights": centred(splits[1], (3, D, D), D ** -0.5, 0.09375, ((1, 16), (2, 16))),
        "out_weights": centred(splits[2], (D, D), D ** -0.5, 0.09375, ((0, 16), (1, 16))),
        "spectrum": centred(splits[3], (2, D, FFT_LEN), 1.0, 6.0, ((1, 16), (2, 16)), jnp.float32),
    }


def reference(tokens, in_weights, out_weights, spectrum):
    outer_gate = jnp.dot(tokens, in_weights[0], preferred_element_type=jnp.float32)
    inner_gate = jnp.dot(tokens, in_weights[1], preferred_element_type=jnp.float32)
    value_proj = jnp.dot(tokens, in_weights[2], preferred_element_type=jnp.float32)
    gated = inner_gate * value_proj
    padded = jnp.concatenate([gated, jnp.zeros_like(gated)], axis=0)
    spectra_in = jnp.fft.fft(padded, axis=0)
    filters = jnp.transpose(spectrum[0]) + 1j * jnp.transpose(spectrum[1])
    convolved = jnp.real(jnp.fft.ifft(spectra_in * filters, axis=0))[:LENGTH]
    convolved = convolved.astype(jnp.float32)
    mixed = (outer_gate * convolved).astype(jnp.bfloat16)
    return jnp.dot(mixed, out_weights, preferred_element_type=jnp.float32).astype(jnp.bfloat16)
```

```python
import functools
import math

import jax
import jax.numpy as jnp
import numpy as np
from jax import lax
from jax.experimental import pallas as pl
from jax.experimental.pallas import tpu as pltpu
from jax.sharding import PartitionSpec as P

MESH = pl.DeviceIdType.MESH
F32 = jnp.float32
BF16 = jnp.bfloat16


def tables():
    p = np.arange(256)[:, None]
    kappa = np.arange(512)[None, :]
    angle = 2.0 * math.pi * ((p * kappa) % 512) / 512.0
    first = np.concatenate([np.cos(angle), -np.sin(angle)], axis=1)
    m0 = np.arange(16)[:, None]
    s = np.arange(16)[None, :]
    turn = np.exp(-2j * math.pi * ((m0 * s) % 16) / 16.0)
    eye = np.eye(16)

    def blocks(table):
        wide = np.kron(table, eye)
        return np.block([[wide.real, -wide.imag], [wide.imag, wide.real]])

    twist = 2.0 * math.pi * m0 * kappa / 8192.0
    rows = np.arange(256)
    perm = np.zeros((256, 256))
    perm[rows, (rows % 16) * 16 + rows // 16] = 1.0
    return (
        jnp.asarray(first, BF16),
        jnp.asarray(blocks(turn), BF16),
        jnp.asarray(blocks(np.conj(turn)), BF16),
        jnp.asarray(np.stack([np.cos(twist), np.sin(twist)]), F32),
        jnp.asarray(perm, BF16),
    )


def swap_blocks(groups):
    lane = lax.broadcasted_iota(jnp.int32, (16, 256), 1) // 16
    for bit in range(4):
        step = 1 << bit
        low = (lane // step) % 2 == 0
        new = list(groups)
        for i in range(16):
            if i & step:
                continue
            j = i | step
            new[i] = jnp.where(low, groups[i], pltpu.roll(groups[j], 16 * step, 1))
            new[j] = jnp.where(low, pltpu.roll(groups[i], 256 - 16 * step, 1), groups[j])
        groups = new
    return groups


def kernel(
    tok, win, wout, spec, first_in, mix_in, unmix_in, twist_in, perm_in, out,
    tbuf, wbuf, obuf, mbuf, sraw, scast, sbuf, gbuf, xbuf, ybuf, rbuf, acc, total,
    first, mix, unmix, twist, perm,
    zt_send, zt_recv, zm_send, zm_recv, w_send, w_recv, o_send, o_recv,
    pair_send, pair_recv, many_send, many_recv, local,
):
    s = lax.axis_index("seq")
    z = lax.axis_index("chan")
    l = lax.axis_index("batch")
    x, h, core = s // 4, (s // 2) % 2, s % 2

    def at_seq(other):
        return {"seq": other}

    def seq_of(x_of, h_of):
        return (x_of % 4) * 4 + h_of * 2 + core

    sibling = at_seq(s + 1 - 2 * core)
    x_up, x_down = at_seq(seq_of(x + 1, h)), at_seq(seq_of(x + 3, h))
    y_same = {"batch": 1 - l}
    y_other = {"seq": seq_of(x, 1 - h), "batch": 1 - l}
    z_up, z_down = {"chan": (z + 1) % 16}, {"chan": (z + 15) % 16}
    sends = []

    barrier = pltpu.get_barrier_semaphore()
    for peer in [at_seq((s + j) % 16) for j in range(1, 16)] + [y_same, y_other, z_up, z_down]:
        pl.semaphore_signal(barrier, inc=1, device_id=peer, device_id_type=MESH)
    pl.semaphore_wait(barrier, 19)

    def remote(src, dst, send, recv, peer):
        return pltpu.make_async_remote_copy(
            src_ref=src, dst_ref=dst, send_sem=send, recv_sem=recv, device_id=peer, device_id_type=MESH
        )

    def ring_send(src, buf, sends_sem, recvs_sem, origin, way, d, p):
        dst = buf.at[origin, pl.ds(128 * p, 128)]
        copy = remote(dst if src is None else src, dst, sends_sem.at[way, d, p], recvs_sem.at[way, d, p],
                      z_up if way == 0 else z_down)
        copy.start()
        sends.append(copy)

    def ring_start(source, buf, sends_sem, recvs_sem):
        for p in range(2):
            for way in range(2):
                src = None if source is None else source.at[pl.ds(128 * p, 128)]
                ring_send(src, buf, sends_sem, recvs_sem, z, way, 0, p)

    def ring_step(buf, sends_sem, recvs_sem, d):
        for p in range(2):
            for way in range(2):
                if d == 8 and p != way:
                    continue
                origin = (z + 16 - d) % 16 if way == 0 else (z + d) % 16
                piece = buf.at[origin, pl.ds(128 * p, 128)]
                remote(piece, piece, sends_sem.at[way, d - 1, p], recvs_sem.at[way, d - 1, p], z_up).wait_recv()
                if d < 7 or (d == 7 and p == way):
                    ring_send(None, buf, sends_sem, recvs_sem, origin, way, d, p)

    def weight_events(source, buf, send, recv, pair):
        def piece(x_of, h_of, half):
            return buf.at[:, pl.ds(pl.multiple_of(seq_of(x_of, h_of) * 256 + half * 128, 128), 128)]

        def hand_on(ref, dst, at, peer):
            copy = remote(ref, dst, send.at[at], recv.at[at], peer)
            copy.start()
            sends.append(copy)

        def to_pair(ref, dst):
            remote(ref, dst, pair_send.at[pair], pair_recv.at[pair], sibling).start()

        def arrive(at, ref):
            remote(ref, ref, send.at[at], recv.at[at], sibling).wait_recv()
            to_pair(ref, ref)

        def start():
            own = lambda half: source.at[:, pl.ds(pl.multiple_of(half * 128, 128), 128)]
            hand_on(own(l), piece(x, h, l), 2, x_up)
            hand_on(own(l), piece(x, h, l), 3, x_down)
            hand_on(own(1 - l), piece(x, h, 1 - l), 0, y_other)
            hand_on(own(l), piece(x, h, l), 1, y_other)
            whole = buf.at[:, pl.ds(pl.multiple_of(s * 256, 256), 256)]
            to_pair(source, whole)
            pltpu.make_async_copy(source, whole, local.at[pair]).start()

        def first_y():
            ref = piece(x, 1 - h, l)
            arrive(0, ref)
            hand_on(ref, ref, 4, x_up)
            hand_on(ref, ref, 5, x_down)

        def first_x():
            ref = piece(x + 3, h, l)
            arrive(2, ref)
            hand_on(ref, ref, 6, x_up)
            hand_on(ref, ref, 8, y_same)
            hand_on(ref, ref, 12, y_other)
            ref = piece(x + 1, h, l)
            arrive(3, ref)
            hand_on(ref, ref, 9, y_same)
            hand_on(ref, ref, 13, y_other)

        def second_x():
            arrive(4, piece(x + 3, 1 - h, l))
            ref = piece(x + 1, 1 - h, l)
            arrive(5, ref)
            hand_on(ref, ref, 7, x_down)

        def second_y():
            arrive(1, piece(x, 1 - h, 1 - l))

        def third_x():
            ref = piece(x + 2, h, l)
            arrive(6, ref)
            hand_on(ref, ref, 10, y_same)
            ref = piece(x + 2, 1 - h, l)
            arrive(7, ref)
            hand_on(ref, ref, 11, y_same)

        def third_y():
            arrive(8, piece(x + 3, h, 1 - l))
            arrive(9, piece(x + 1, h, 1 - l))

        def fourth_y():
            arrive(12, piece(x + 3, 1 - h, 1 - l))
            arrive(13, piece(x + 1, 1 - h, 1 - l))

        def fifth_y():
            arrive(10, piece(x + 2, h, 1 - l))
            arrive(11, piece(x + 2, 1 - h, 1 - l))

        half_all = buf.at[:, pl.ds(0, 2048)]

        def finish():
            whole = buf.at[:, pl.ds(pl.multiple_of(s * 256, 256), 256)]
            pltpu.make_async_copy(source, whole, local.at[pair]).wait()
            remote(half_all, half_all, pair_send.at[pair], pair_recv.at[pair], sibling).wait_recv()

        def drain():
            remote(half_all, half_all, pair_send.at[pair], pair_recv.at[pair], sibling).wait_send()

        return (start, first_y, first_x, second_x, second_y, third_x, third_y, fourth_y, fifth_y, finish, drain)

    def spread(source, dest, at):
        for j in range(1, 16):
            peer = (s + j) % 16
            remote(source(peer), dest, many_send.at[at], many_recv.at[at], at_seq(peer)).start()

    def collect(ref, at):
        remote(ref, ref, many_send.at[at], many_recv.at[at], sibling).wait_recv()

    def drain_many(ref, at):
        remote(ref, ref, many_send.at[at], many_recv.at[at], sibling).wait_send()

    w = weight_events(win, wbuf, w_send, w_recv, 0)
    o = weight_events(wout, obuf, o_send, o_recv, 1)

    ring_start(tok, tbuf, zt_send, zt_recv)
    w[0]()
    own_tokens = pltpu.make_async_copy(tok, tbuf.at[z], local.at[2])
    own_tokens.start()
    raw = pltpu.make_async_copy(spec, sraw, local.at[3])
    raw.start()
    loads = [
        pltpu.make_async_copy(src, dst, local.at[4 + at])
        for at, (src, dst) in enumerate(
            ((first_in, first), (mix_in, mix), (unmix_in, unmix), (twist_in, twist), (perm_in, perm))
        )
    ]
    for load in loads:
        load.start()
    raw.wait()
    scast[...] = sraw[...].astype(BF16)

    def step_t(d):
        ring_step(tbuf, zt_send, zt_recv, d)

    step_t(1)
    w[1]()
    w[2]()
    step_t(2)

    def rows16(ref, at):
        return ref.at[:, pl.ds(pl.multiple_of(at * 16, 16), 16)]

    mine = rows16(sbuf, s)
    spread(lambda peer: rows16(scast, peer), mine, 0)
    own_rows = pl.ds(pl.multiple_of(s * 16, 16), 16)
    sbuf[:, own_rows, :] = scast[:, own_rows, :]
    step_t(3)
    w[3]()
    w[4]()
    step_t(4)
    w[5]()
    step_t(5)
    w[6]()
    step_t(6)
    w[7]()
    step_t(7)
    w[8]()
    own_tokens.wait()
    w[9]()

    acc[...] = jnp.zeros_like(acc)

    def project(origin):
        block = tbuf[origin]
        rows = pl.ds(pl.multiple_of(origin * 256, 256), 256)
        for j in range(3):
            acc[j] += jnp.dot(block, wbuf[j, rows, :], preferred_element_type=F32)

    project(z)
    for d in range(1, 8):
        project((z + 16 - d) % 16)
        project((z + d) % 16)
    step_t(8)
    project((z + 8) % 16)

    for load in loads:
        load.wait()
    gated = (acc[1] * acc[2]).astype(BF16)
    gated = jnp.dot(perm[...], gated, preferred_element_type=F32)
    groups = swap_blocks([gated[16 * i : 16 * i + 16, :] for i in range(16)])
    for i in range(16):
        gbuf[i] = groups[i].astype(BF16)
    spread(lambda peer: gbuf.at[peer], xbuf.at[s], 1)
    xbuf[s] = gbuf[s]
    collect(sbuf.at[:, pl.ds(0, 240)], 0)
    collect(xbuf.at[pl.ds(0, 15)], 1)

    signal = xbuf[...].reshape(256, 256).astype(F32).T.astype(BF16)
    spectrum = jnp.dot(signal, first[...], preferred_element_type=F32)
    a_re = spectrum[:, :512].reshape(16, 16, 512)
    a_im = spectrum[:, 512:].reshape(16, 16, 512)
    cos, sin = twist[0][:, None, :], twist[1][:, None, :]
    b_re = (a_re * cos + a_im * sin).reshape(256, 512)
    b_im = (a_im * cos - a_re * sin).reshape(256, 512)
    b = jnp.concatenate([b_re, b_im], axis=0).astype(BF16)
    u = jnp.dot(mix[...], b, preferred_element_type=F32)
    u_re, u_im = u[:256], u[256:]
    f_re, f_im = sbuf[0].astype(F32), sbuf[1].astype(F32)
    v = jnp.concatenate([u_re * f_re - u_im * f_im, u_re * f_im + u_im * f_re], axis=0).astype(BF16)
    c = jnp.dot(unmix[...], v, preferred_element_type=F32)
    c_re, c_im = c[:256].reshape(16, 16, 512), c[256:].reshape(16, 16, 512)
    d_re = (c_re * cos - c_im * sin).reshape(256, 512)
    d_im = (c_im * cos + c_re * sin).reshape(256, 512)
    d_all = jnp.concatenate([d_re, d_im], axis=1).astype(BF16)
    y = lax.dot_general(first[...], d_all, (((1,), (1,)), ((), ())), preferred_element_type=F32)
    ybuf[...] = (y * (1.0 / 8192.0)).astype(BF16).reshape(16, 16, 256)
    spread(lambda peer: ybuf.at[peer], rbuf.at[s], 2)
    rbuf[s] = ybuf[s]
    collect(rbuf.at[pl.ds(0, 15)], 2)

    groups = swap_blocks([rbuf[i].astype(F32) for i in range(16)])
    conv = jnp.concatenate(groups, axis=0).astype(BF16)
    conv = jnp.dot(perm[...], conv, preferred_element_type=F32)
    mbuf[z] = (acc[0] * conv).astype(BF16)

    ring_start(None, mbuf, zm_send, zm_recv)
    o[0]()
    total[...] = jnp.zeros_like(total)

    def step_m(d):
        ring_step(mbuf, zm_send, zm_recv, d)

    def combine(origin):
        rows = pl.ds(pl.multiple_of(origin * 256, 256), 256)
        total[...] += jnp.dot(mbuf[origin], obuf[0, rows, :], preferred_element_type=F32)

    step_m(1)
    o[1]()
    o[2]()
    step_m(2)
    o[3]()
    o[4]()
    o[5]()
    step_m(3)
    o[6]()
    o[7]()
    step_m(4)
    o[8]()
    o[9]()
    step_m(5)
    combine(z)
    for d in range(1, 8):
        if d > 5:
            step_m(d)
        combine((z + 16 - d) % 16)
        combine((z + d) % 16)
    step_m(8)
    combine((z + 8) % 16)
    out[...] = total[...].astype(BF16)

    for copy in sends:
        copy.wait_send()
    w[10]()
    o[10]()
    drain_many(sbuf.at[:, pl.ds(0, 240)], 0)
    drain_many(xbuf.at[pl.ds(0, 15)], 1)
    drain_many(rbuf.at[pl.ds(0, 15)], 2)


def body(tokens, in_weights, out_weights, spectrum):
    dma = pltpu.SemaphoreType.DMA
    any_spec = pl.BlockSpec(memory_space=pl.ANY)
    return pl.pallas_call(
        kernel,
        out_shape=jax.ShapeDtypeStruct((256, 256), BF16),
        in_specs=[any_spec] * 9,
        out_specs=pl.BlockSpec(memory_space=pltpu.VMEM),
        scratch_shapes=[
            pltpu.VMEM((16, 256, 256), BF16),
            pltpu.VMEM((3, 4096, 256), BF16),
            pltpu.VMEM((1, 4096, 256), BF16),
            pltpu.VMEM((16, 256, 256), BF16),
            pltpu.VMEM((2, 256, 512), F32),
            pltpu.VMEM((2, 256, 512), BF16),
            pltpu.VMEM((2, 256, 512), BF16),
            pltpu.VMEM((16, 16, 256), BF16),
            pltpu.VMEM((16, 16, 256), BF16),
            pltpu.VMEM((16, 16, 256), BF16),
            pltpu.VMEM((16, 16, 256), BF16),
            pltpu.VMEM((3, 256, 256), F32),
            pltpu.VMEM((256, 256), F32),
            pltpu.VMEM((256, 1024), BF16),
            pltpu.VMEM((512, 512), BF16),
            pltpu.VMEM((512, 512), BF16),
            pltpu.VMEM((2, 16, 512), F32),
            pltpu.VMEM((256, 256), BF16),
            dma((2, 8, 2)),
            dma((2, 8, 2)),
            dma((2, 8, 2)),
            dma((2, 8, 2)),
            dma((14,)),
            dma((14,)),
            dma((14,)),
            dma((14,)),
            dma((2,)),
            dma((2,)),
            dma((3,)),
            dma((3,)),
            dma((9,)),
        ],
        compiler_params=pltpu.CompilerParams(
            collective_id=0, has_side_effects=True, vmem_limit_bytes=48 * 1024 * 1024
        ),
    )(tokens, in_weights, out_weights[None], spectrum, *tables())


def solution(mesh):
    placed = (
        P(("batch", "seq"), "chan"),
        P(None, "seq", "chan"),
        P("seq", "chan"),
        P(None, "chan", "seq"),
    )
    return jax.shard_map(
        body, mesh=mesh, in_specs=placed, out_specs=P(("batch", "seq"), "chan"), check_vma=False
    )
```

```python
import math

import jax
import jax.numpy as jnp
import numpy as np
from jax import lax
from jax.experimental import pallas as pl
from jax.experimental.pallas import tpu as pltpu
from jax.sharding import PartitionSpec as P

MESH = pl.DeviceIdType.MESH
F32 = jnp.float32
BF16 = jnp.bfloat16


def tables():
    p = np.arange(256)[:, None]
    kappa = np.arange(512)[None, :]
    angle = 2.0 * math.pi * ((p * kappa) % 512) / 512.0
    m0 = np.arange(16)[:, None]
    s = np.arange(16)[None, :]
    turn = np.exp(-2j * math.pi * ((m0 * s) % 16) / 16.0)

    def blocks(table):
        wide = np.kron(table, np.eye(8))
        return np.block([[wide.real, -wide.imag], [wide.imag, wide.real]])

    twist = 2.0 * math.pi * m0 * kappa / 8192.0
    rows = np.arange(256)
    by_m0 = np.eye(256)[(rows % 16) * 16 + rows // 16]
    by_owner = np.eye(256)[(rows // 8 % 2) * 128 + rows // 16 * 8 + rows % 8]
    wide = [np.cos(angle), -np.sin(angle), blocks(turn), blocks(np.conj(turn)), by_m0, by_owner]
    return (
        jnp.asarray(np.concatenate(wide, axis=1), BF16),
        jnp.asarray(np.stack([np.cos(twist), np.sin(twist)]), F32),
    )


def swap_blocks(groups):
    lane = lax.broadcasted_iota(jnp.int32, (16, 128), 1) // 8
    for bit in range(4):
        step = 1 << bit
        low = (lane // step) % 2 == 0
        new = list(groups)
        for i in range(16):
            if i & step:
                continue
            j = i | step
            new[i] = jnp.where(low, groups[i], pltpu.roll(groups[j], 8 * step, 1))
            new[j] = jnp.where(low, pltpu.roll(groups[i], 128 - 8 * step, 1), groups[j])
        groups = new
    return groups


def kernel(
    tok, win, wout, spec, table_in, twist_in, out,
    tbuf, wbuf, obuf, mbuf, sraw, scast, sbuf, gbuf, xbuf, ybuf, rbuf, acc, total, table, twist,
    zt_send, zt_recv, zm_send, zm_recv, w_send, w_recv, pair_send, pair_recv, many_send, many_recv, local,
):
    s = lax.axis_index("seq")
    z = lax.axis_index("chan")
    l = lax.axis_index("batch")
    x, h, core = s // 4, (s // 2) % 2, s % 2

    def at_seq(other):
        return {"seq": other}

    def seq_of(x_of, h_of):
        return (x_of % 4) * 4 + h_of * 2 + core

    sibling = at_seq(s + 1 - 2 * core)
    x_up, x_down = at_seq(seq_of(x + 1, h)), at_seq(seq_of(x + 3, h))
    y_same = {"batch": 1 - l}
    y_other = {"seq": seq_of(x, 1 - h), "batch": 1 - l}
    z_at = lambda step: {"chan": (z + 16 + step) % 16}
    sends = []

    barrier = pltpu.get_barrier_semaphore()
    peers = [at_seq((s + j) % 16) for j in range(1, 16)] + [y_same, y_other] + [z_at(step) for step in (1, -1, 2, -2)]
    for peer in peers:
        pl.semaphore_signal(barrier, inc=1, device_id=peer, device_id_type=MESH)
    raw = pltpu.make_async_copy(spec, sraw, local.at[8])
    loads = [
        pltpu.make_async_copy(table_in, table, local.at[9]),
        pltpu.make_async_copy(twist_in, twist, local.at[10]),
    ]
    for load in [raw] + loads:
        load.start()
    pl.semaphore_wait(barrier, len(peers))

    def remote(src, dst, send, recv, peer):
        return pltpu.make_async_remote_copy(
            src_ref=src, dst_ref=dst, send_sem=send, recv_sem=recv, device_id=peer, device_id_type=MESH
        )

    def ring(source, buf, sends_sem, recvs_sem):
        def send(origin, way, d, p, step):
            dst = buf.at[origin, p]
            src = source.at[pl.ds(64 * p, 64)] if d == 1 and source is not None else dst
            peer = z_at(step if way == 0 else -step)
            copy = remote(src, dst, sends_sem.at[way, d - 1, p], recvs_sem.at[way, d - 1, p], peer)
            copy.start()
            sends.append(copy)

        def start(pieces):
            for p in pieces:
                for way in range(2):
                    send(z, way, 1, p, 1)

        def take(d, p):
            for way in range(2):
                if d == 8 and p % 2 != way:
                    continue
                origin = (z + 16 - d) % 16 if way == 0 else (z + d) % 16
                piece = buf.at[origin, p]
                remote(piece, piece, sends_sem.at[way, d - 1, p], recvs_sem.at[way, d - 1, p], z_at(1)).wait_recv()
                if d < 7:
                    send(origin, way, d + 1, p, 1)
                if d == 6 and p % 2 == way:
                    send(origin, way, 8, p, 2)

        return start, take

    def weight_events(source, buf, pair):
        def piece(x_of, h_of, half):
            return buf.at[pl.ds(pl.multiple_of(seq_of(x_of, h_of) * 256 + half * 128, 128), 128)]

        def hand_on(ref, dst, at, peer):
            copy = remote(ref, dst, w_send.at[pair, at], w_recv.at[pair, at], peer)
            copy.start()
            sends.append(copy)

        def to_pair(ref, dst):
            remote(ref, dst, pair_send.at[pair], pair_recv.at[pair], sibling).start()

        def arrive(at, ref):
            remote(ref, ref, w_send.at[pair, at], w_recv.at[pair, at], sibling).wait_recv()
            to_pair(ref, ref)

        def start():
            own = lambda half: source.at[pl.ds(pl.multiple_of(half * 128, 128), 128)]
            hand_on(own(l), piece(x, h, l), 2, x_up)
            hand_on(own(l), piece(x, h, l), 3, x_down)
            hand_on(own(1 - l), piece(x, h, 1 - l), 0, y_other)
            hand_on(own(l), piece(x, h, l), 1, y_other)
            whole = buf.at[pl.ds(pl.multiple_of(s * 256, 256), 256)]
            to_pair(source, whole)
            pltpu.make_async_copy(source, whole, local.at[pair]).start()

        def y1():
            ref = piece(x, 1 - h, l)
            arrive(0, ref)
            hand_on(ref, ref, 4, x_up)
            hand_on(ref, ref, 5, x_down)

        def x1():
            ref = piece(x + 3, h, l)
            arrive(2, ref)
            hand_on(ref, ref, 6, x_up)
            hand_on(ref, ref, 8, y_same)
            hand_on(ref, ref, 12, y_other)
            ref = piece(x + 1, h, l)
            arrive(3, ref)
            hand_on(ref, ref, 9, y_same)
            hand_on(ref, ref, 13, y_other)

        def y2():
            arrive(1, piece(x, 1 - h, 1 - l))

        def x2():
            ref = piece(x + 1, 1 - h, l)
            arrive(5, ref)
            hand_on(ref, ref, 7, x_down)

        def x3():
            arrive(4, piece(x + 3, 1 - h, l))

        def x4():
            ref = piece(x + 2, h, l)
            arrive(6, ref)
            hand_on(ref, ref, 10, y_same)

        def x5():
            ref = piece(x + 2, 1 - h, l)
            arrive(7, ref)
            hand_on(ref, ref, 11, y_same)

        def y3():
            arrive(8, piece(x + 3, h, 1 - l))
            arrive(9, piece(x + 1, h, 1 - l))

        def y4():
            arrive(12, piece(x + 3, 1 - h, 1 - l))
            arrive(13, piece(x + 1, 1 - h, 1 - l))

        def y5():
            arrive(10, piece(x + 2, h, 1 - l))
            arrive(11, piece(x + 2, 1 - h, 1 - l))

        half_all = buf.at[pl.ds(0, 2048)]

        def finish():
            whole = buf.at[pl.ds(pl.multiple_of(s * 256, 256), 256)]
            pltpu.make_async_copy(source, whole, local.at[pair]).wait()
            remote(half_all, half_all, pair_send.at[pair], pair_recv.at[pair], sibling).wait_recv()

        def drain():
            remote(half_all, half_all, pair_send.at[pair], pair_recv.at[pair], sibling).wait_send()

        steps = (start, y1, x1, y2, x2, x3, x4, x5, y3, y4, y5, finish, drain)
        return {step.__name__: step for step in steps}

    def spread(source, dest, at):
        for j in range(1, 16):
            peer = (s + j) % 16
            remote(source(peer), dest, many_send.at[at], many_recv.at[at], at_seq(peer)).start()

    def collect(ref, at):
        remote(ref, ref, many_send.at[at], many_recv.at[at], sibling).wait_recv()

    def drain_many(ref, at):
        remote(ref, ref, many_send.at[at], many_recv.at[at], sibling).wait_send()

    w = [weight_events(win.at[j], wbuf.at[j], j) for j in range(3)]
    o = weight_events(wout, obuf, 3)

    start_t, take_t = ring(tok, tbuf, zt_send, zt_recv)
    start_m, take_m = ring(None, mbuf, zm_send, zm_recv)

    start_t(range(4))
    for j in (1, 2, 0):
        w[j]["start"]()
    own_tokens = [
        pltpu.make_async_copy(tok.at[pl.ds(64 * p, 64)], tbuf.at[z, p], local.at[4 + p]) for p in range(4)
    ]
    for load in own_tokens:
        load.start()
    raw.wait()
    for load in loads:
        load.wait()
    for part in range(2):
        rows = jnp.dot(table[:, 1792:], sraw[part].astype(BF16), preferred_element_type=F32)
        scast[part] = rows.astype(BF16)

    def rows16(ref, at):
        return ref.at[:, pl.ds(pl.multiple_of(at * 16, 16), 16)]

    def spread_spectrum():
        spread(lambda peer: rows16(scast, peer), rows16(sbuf, s), 0)
        own_rows = pl.ds(pl.multiple_of(s * 16, 16), 16)
        sbuf[:, own_rows, :] = scast[:, own_rows, :]

    plan = {
        (1, 2): "1y1 1x1",
        (1, 3): "2y1 2x1",
        (2, 1): "0y1 0x1",
        (2, 3): "1y2 1x2",
        (3, 0): "2y2 1x3",
        (3, 1): "1x4 1y3",
        (3, 2): "2x2 0y2",
        (3, 3): "0x2 2x3",
        (4, 0): "1x5 2y3",
        (4, 1): "2x4 1y4",
        (4, 2): "0x3",
        (4, 3): "2x5",
        (5, 0): "0x4 0x5 0y3",
        (5, 1): "2y4",
        (6, 0): "0y4 1y5",
        (6, 3): "2y5",
        (7, 2): "0y5",
    }
    for d in range(1, 8):
        for p in range(4):
            take_t(d, p)
            for word in plan.get((d, p), "").split():
                w[int(word[0])][word[1:]]()
            if (d, p) == (5, 2):
                spread_spectrum()
    for load in own_tokens:
        load.wait()
    w[1]["finish"]()
    w[2]["finish"]()

    def project(origin, which, fresh=False):
        block = tbuf[origin].reshape(256, 256)
        rows = pl.ds(pl.multiple_of(origin * 256, 256), 256)
        for j in which:
            part = jnp.dot(block, wbuf[j, rows, :], preferred_element_type=F32)
            acc[j] = part if fresh else acc[j] + part

    def project_near(which):
        project(z, which, True)
        for d in range(1, 8):
            project((z + 16 - d) % 16, which)
            project((z + d) % 16, which)

    project_near((1, 2))
    for p in range(4):
        take_t(8, p)
    project((z + 8) % 16, (1, 2))

    by_m0 = table[:, 1536:1792]
    for half in range(2):
        lanes = slice(128 * half, 128 * half + 128)
        gated = (acc[1, :, lanes] * acc[2, :, lanes]).astype(BF16)
        gated = jnp.dot(by_m0, gated, preferred_element_type=F32)
        groups = swap_blocks([gated[16 * i : 16 * i + 16, :] for i in range(16)])
        for i in range(16):
            gbuf[half, i] = groups[i].astype(BF16)
        spread(lambda peer: gbuf.at[half, peer], xbuf.at[half, s], 1 + half)
        xbuf[half, s] = gbuf[half, s]

    w[0]["finish"]()
    project_near((0,))
    project((z + 8) % 16, (0,))
    collect(sbuf.at[:, pl.ds(0, 240)], 0)

    cos, sin = twist[0][:, None, :], twist[1][:, None, :]
    first, mix, unmix = table[:, :1024], table[:, 1024:1280], table[:, 1280:1536]
    for half in range(2):
        collect(xbuf.at[half, pl.ds(0, 15)], 1 + half)
        signal = xbuf[half].reshape(256, 128).astype(F32).T.astype(BF16)
        a = jnp.dot(signal, first, preferred_element_type=F32)
        a_re, a_im = a[:, :512].reshape(16, 8, 512), a[:, 512:].reshape(16, 8, 512)
        b_re = (a_re * cos + a_im * sin).reshape(128, 512)
        b_im = (a_im * cos - a_re * sin).reshape(128, 512)
        b = jnp.concatenate([b_re, b_im], axis=0).astype(BF16)
        u = jnp.dot(mix, b, preferred_element_type=F32)
        u_re, u_im = u[:128], u[128:]
        f_re, f_im = (
            sbuf[part].astype(F32).reshape(16, 2, 8, 512)[:, half].reshape(128, 512) for part in range(2)
        )
        v = jnp.concatenate([u_re * f_re - u_im * f_im, u_re * f_im + u_im * f_re], axis=0).astype(BF16)
        c = jnp.dot(unmix, v, preferred_element_type=F32)
        c_re, c_im = c[:128].reshape(16, 8, 512), c[128:].reshape(16, 8, 512)
        d_re = (c_re * cos - c_im * sin).reshape(128, 512)
        d_im = (c_im * cos + c_re * sin).reshape(128, 512)
        d_all = jnp.concatenate([d_re, d_im], axis=1).astype(BF16)
        y = lax.dot_general(first, d_all, (((1,), (1,)), ((), ())), preferred_element_type=F32)
        ybuf[half] = (y * (1.0 / 8192.0)).astype(BF16).reshape(16, 16, 128)
        spread(lambda peer: ybuf.at[half, peer], rbuf.at[half, s], 3 + half)
        rbuf[half, s] = ybuf[half, s]

    for half in range(2):
        collect(rbuf.at[half, pl.ds(0, 15)], 3 + half)
        groups = swap_blocks([rbuf[half, i].astype(F32) for i in range(16)])
        conv = jnp.concatenate(groups, axis=0).astype(BF16)
        conv = jnp.dot(by_m0, conv, preferred_element_type=F32)
        mixed = (acc[0, :, 128 * half : 128 * half + 128] * conv).astype(BF16)
        mbuf[z, 2 * half] = mixed[:128]
        mbuf[z, 2 * half + 1] = mixed[128:]
        start_m((2 * half, 2 * half + 1))

    o["start"]()
    total[...] = jnp.zeros_like(total)

    def combine(origin):
        for half in range(2):
            rows = pl.ds(pl.multiple_of(origin * 256 + 128 * half, 128), 128)
            block = jnp.concatenate([mbuf[origin, 2 * half], mbuf[origin, 2 * half + 1]], axis=0)
            total[...] += jnp.dot(block, obuf[rows, :], preferred_element_type=F32)

    plan = {
        (1, 2): "y1 x1",
        (2, 0): "y2",
        (2, 3): "x2 x3",
        (3, 1): "x4 y3 y4",
        (4, 0): "x5",
        (5, 1): "y5",
        (5, 3): "finish",
    }
    for d in range(1, 8):
        for p in range(4):
            take_m(d, p)
            for word in plan.get((d, p), "").split():
                o[word]()
        if d == 6:
            combine(z)
            for near in range(1, 4):
                combine((z + 16 - near) % 16)
                combine((z + near) % 16)
    for near in range(4, 8):
        combine((z + 16 - near) % 16)
        combine((z + near) % 16)
    for p in range(4):
        take_m(8, p)
    combine((z + 8) % 16)
    out[...] = total[...].astype(BF16)

    for copy in sends:
        copy.wait_send()
    for each in w + [o]:
        each["drain"]()
    drain_many(sbuf.at[:, pl.ds(0, 240)], 0)
    for half in range(2):
        drain_many(xbuf.at[half, pl.ds(0, 15)], 1 + half)
        drain_many(rbuf.at[half, pl.ds(0, 15)], 3 + half)


def body(tokens, in_weights, out_weights, spectrum):
    dma = pltpu.SemaphoreType.DMA
    any_spec = pl.BlockSpec(memory_space=pl.ANY)
    return pl.pallas_call(
        kernel,
        out_shape=jax.ShapeDtypeStruct((256, 256), BF16),
        in_specs=[any_spec] * 6,
        out_specs=pl.BlockSpec(memory_space=pltpu.VMEM),
        scratch_shapes=[
            pltpu.VMEM((16, 4, 64, 256), BF16),
            pltpu.VMEM((3, 4096, 256), BF16),
            pltpu.VMEM((4096, 256), BF16),
            pltpu.VMEM((16, 4, 128, 128), BF16),
            pltpu.VMEM((2, 256, 512), F32),
            pltpu.VMEM((2, 256, 512), BF16),
            pltpu.VMEM((2, 256, 512), BF16),
            pltpu.VMEM((2, 16, 16, 128), BF16),
            pltpu.VMEM((2, 16, 16, 128), BF16),
            pltpu.VMEM((2, 16, 16, 128), BF16),
            pltpu.VMEM((2, 16, 16, 128), BF16),
            pltpu.VMEM((3, 256, 256), F32),
            pltpu.VMEM((256, 256), F32),
            pltpu.VMEM((256, 2048), BF16),
            pltpu.VMEM((2, 16, 512), F32),
            dma((2, 8, 4)),
            dma((2, 8, 4)),
            dma((2, 8, 4)),
            dma((2, 8, 4)),
            dma((4, 14)),
            dma((4, 14)),
            dma((4,)),
            dma((4,)),
            dma((5,)),
            dma((5,)),
            dma((11,)),
        ],
        compiler_params=pltpu.CompilerParams(
            collective_id=0, has_side_effects=True, vmem_limit_bytes=60 * 1024 * 1024
        ),
    )(tokens, in_weights, out_weights, spectrum, *tables())


def solution(mesh):
    placed = (
        P(("batch", "seq"), "chan"),
        P(None, "seq", "chan"),
        P("seq", "chan"),
        P(None, "chan", "seq"),
    )
    return jax.shard_map(
        body, mesh=mesh, in_specs=placed, out_specs=P(("batch", "seq"), "chan"), check_vma=False
    )
```

```python
import math

import jax
import jax.numpy as jnp
import numpy as np
from jax import lax
from jax.experimental import pallas as pl
from jax.experimental.pallas import tpu as pltpu
from jax.sharding import PartitionSpec as P

MESH = pl.DeviceIdType.MESH
F32 = jnp.float32
BF16 = jnp.bfloat16


def tables():
    p = np.arange(256)[:, None]
    kappa = np.arange(512)[None, :]
    angle = 2.0 * math.pi * ((p * kappa) % 512) / 512.0
    m0 = np.arange(16)[:, None]
    s = np.arange(16)[None, :]
    turn = np.exp(-2j * math.pi * ((m0 * s) % 16) / 16.0)

    def blocks(table):
        wide = np.kron(table, np.eye(8))
        return np.block([[wide.real, -wide.imag], [wide.imag, wide.real]])

    twist = 2.0 * math.pi * m0 * kappa / 8192.0
    rows = np.arange(256)
    by_m0 = np.eye(256)[(rows % 16) * 16 + rows // 16]
    by_owner = np.eye(256)[(rows // 8 % 2) * 128 + rows // 16 * 8 + rows % 8]
    wide = [np.cos(angle), -np.sin(angle), blocks(turn), blocks(np.conj(turn)), by_m0, by_owner]
    return (
        jnp.asarray(np.concatenate(wide, axis=1), BF16),
        jnp.asarray(np.stack([np.cos(twist), np.sin(twist)]), F32),
    )


def swap_blocks(groups):
    lane = lax.broadcasted_iota(jnp.int32, (16, 128), 1) // 8
    for bit in range(4):
        step = 1 << bit
        low = (lane // step) % 2 == 0
        new = list(groups)
        for i in range(16):
            if i & step:
                continue
            j = i | step
            new[i] = jnp.where(low, groups[i], pltpu.roll(groups[j], 8 * step, 1))
            new[j] = jnp.where(low, pltpu.roll(groups[i], 128 - 8 * step, 1), groups[j])
        groups = new
    return groups


def kernel(
    tok, win, wout, spec, table_in, twist_in, out,
    tbuf, wbuf, obuf, mbuf, sraw, scast, sbuf, gbuf, xbuf, ybuf, rbuf, acc, total, table, twist,
    zt_send, zt_recv, zm_send, zm_recv, w_send, w_recv, pair_send, pair_recv, many_send, many_recv, local,
):
    s = lax.axis_index("seq")
    z = lax.axis_index("chan")
    l = lax.axis_index("batch")
    x, h, core = s // 4, (s // 2) % 2, s % 2

    def at_seq(other):
        return {"seq": other}

    def seq_of(x_of, h_of):
        return (x_of % 4) * 4 + h_of * 2 + core

    sibling = at_seq(s + 1 - 2 * core)
    x_up, x_down = at_seq(seq_of(x + 1, h)), at_seq(seq_of(x + 3, h))
    y_same = {"batch": 1 - l}
    y_other = {"seq": seq_of(x, 1 - h), "batch": 1 - l}
    z_at = lambda step: {"chan": (z + 16 + step) % 16}
    sends = []

    barrier = pltpu.get_barrier_semaphore()
    peers = [at_seq((s + j) % 16) for j in range(1, 16)] + [y_same, y_other] + [z_at(step) for step in (1, -1, 2, -2)]
    for peer in peers:
        pl.semaphore_signal(barrier, inc=1, device_id=peer, device_id_type=MESH)
    raw = pltpu.make_async_copy(spec, sraw, local.at[8])
    loads = [
        pltpu.make_async_copy(table_in, table, local.at[9]),
        pltpu.make_async_copy(twist_in, twist, local.at[10]),
    ]
    for load in [raw] + loads:
        load.start()
    pl.semaphore_wait(barrier, len(peers))

    def remote(src, dst, send, recv, peer):
        return pltpu.make_async_remote_copy(
            src_ref=src, dst_ref=dst, send_sem=send, recv_sem=recv, device_id=peer, device_id_type=MESH
        )

    def ring(source, buf, sends_sem, recvs_sem):
        def send(origin, way, d, p, step):
            dst = buf.at[origin, p]
            src = source.at[pl.ds(64 * p, 64)] if d == 1 and source is not None else dst
            peer = z_at(step if way == 0 else -step)
            copy = remote(src, dst, sends_sem.at[way, d - 1, p], recvs_sem.at[way, d - 1, p], peer)
            copy.start()
            sends.append(copy)

        def start(pieces):
            for p in pieces:
                for way in range(2):
                    send(z, way, 1, p, 1)

        def take(d, p):
            for way in range(2):
                if d == 8 and p % 2 != way:
                    continue
                origin = (z + 16 - d) % 16 if way == 0 else (z + d) % 16
                piece = buf.at[origin, p]
                remote(piece, piece, sends_sem.at[way, d - 1, p], recvs_sem.at[way, d - 1, p], z_at(1)).wait_recv()
                if d < 7:
                    send(origin, way, d + 1, p, 1)
                if d == 6 and p % 2 == way:
                    send(origin, way, 8, p, 2)

        return start, take

    def weight_events(source, buf, pair):
        def piece(x_of, h_of, half):
            return buf.at[pl.ds(pl.multiple_of(seq_of(x_of, h_of) * 256 + half * 128, 128), 128)]

        def hand_on(ref, dst, at, peer):
            copy = remote(ref, dst, w_send.at[pair, at], w_recv.at[pair, at], peer)
            copy.start()
            sends.append(copy)

        def to_pair(ref, dst):
            remote(ref, dst, pair_send.at[pair], pair_recv.at[pair], sibling).start()

        def arrive(at, ref):
            remote(ref, ref, w_send.at[pair, at], w_recv.at[pair, at], sibling).wait_recv()
            to_pair(ref, ref)

        def start():
            own = lambda half: source.at[pl.ds(pl.multiple_of(half * 128, 128), 128)]
            hand_on(own(l), piece(x, h, l), 2, x_up)
            hand_on(own(l), piece(x, h, l), 3, x_down)
            hand_on(own(1 - l), piece(x, h, 1 - l), 0, y_other)
            hand_on(own(l), piece(x, h, l), 1, y_other)
            whole = buf.at[pl.ds(pl.multiple_of(s * 256, 256), 256)]
            to_pair(source, whole)
            pltpu.make_async_copy(source, whole, local.at[pair]).start()

        def y1():
            ref = piece(x, 1 - h, l)
            arrive(0, ref)
            hand_on(ref, ref, 4, x_up)
            hand_on(ref, ref, 5, x_down)

        def x1():
            ref = piece(x + 3, h, l)
            arrive(2, ref)
            hand_on(ref, ref, 6, x_up)
            hand_on(ref, ref, 8, y_same)
            hand_on(ref, ref, 12, y_other)
            ref = piece(x + 1, h, l)
            arrive(3, ref)
            hand_on(ref, ref, 9, y_same)
            hand_on(ref, ref, 13, y_other)

        def y2():
            arrive(1, piece(x, 1 - h, 1 - l))

        def x2():
            ref = piece(x + 1, 1 - h, l)
            arrive(5, ref)
            hand_on(ref, ref, 7, x_down)

        def x3():
            arrive(4, piece(x + 3, 1 - h, l))

        def x4():
            ref = piece(x + 2, h, l)
            arrive(6, ref)
            hand_on(ref, ref, 10, y_same)

        def x5():
            ref = piece(x + 2, 1 - h, l)
            arrive(7, ref)
            hand_on(ref, ref, 11, y_same)

        def y3():
            arrive(8, piece(x + 3, h, 1 - l))
            arrive(9, piece(x + 1, h, 1 - l))

        def y4():
            arrive(12, piece(x + 3, 1 - h, 1 - l))
            arrive(13, piece(x + 1, 1 - h, 1 - l))

        def y5():
            arrive(10, piece(x + 2, h, 1 - l))
            arrive(11, piece(x + 2, 1 - h, 1 - l))

        half_all = buf.at[pl.ds(0, 2048)]

        def finish():
            whole = buf.at[pl.ds(pl.multiple_of(s * 256, 256), 256)]
            pltpu.make_async_copy(source, whole, local.at[pair]).wait()
            remote(half_all, half_all, pair_send.at[pair], pair_recv.at[pair], sibling).wait_recv()

        def drain():
            remote(half_all, half_all, pair_send.at[pair], pair_recv.at[pair], sibling).wait_send()

        steps = (start, y1, x1, y2, x2, x3, x4, x5, y3, y4, y5, finish, drain)
        return {step.__name__: step for step in steps}

    def spread(source, dest, at):
        for j in range(1, 16):
            peer = (s + j) % 16
            remote(source(peer), dest, many_send.at[at], many_recv.at[at], at_seq(peer)).start()

    def collect(ref, at):
        remote(ref, ref, many_send.at[at], many_recv.at[at], sibling).wait_recv()

    def drain_many(ref, at):
        remote(ref, ref, many_send.at[at], many_recv.at[at], sibling).wait_send()

    w = [weight_events(win.at[j], wbuf.at[j], j) for j in range(3)]
    o = weight_events(wout, obuf, 3)

    start_t, take_t = ring(tok, tbuf, zt_send, zt_recv)
    start_m, take_m = ring(None, mbuf, zm_send, zm_recv)

    start_t(range(4))
    for j in (1, 2, 0):
        w[j]["start"]()
    own_tokens = [
        pltpu.make_async_copy(tok.at[pl.ds(64 * p, 64)], tbuf.at[z, p], local.at[4 + p]) for p in range(4)
    ]
    for load in own_tokens:
        load.start()
    raw.wait()
    for load in loads:
        load.wait()
    for part in range(2):
        rows = jnp.dot(table[:, 1792:], sraw[part].astype(BF16), preferred_element_type=F32)
        scast[part] = rows.astype(BF16)

    def rows16(ref, at):
        return ref.at[:, pl.ds(pl.multiple_of(at * 16, 16), 16)]

    def spread_spectrum():
        spread(lambda peer: rows16(scast, peer), rows16(sbuf, s), 0)
        own_rows = pl.ds(pl.multiple_of(s * 16, 16), 16)
        sbuf[:, own_rows, :] = scast[:, own_rows, :]

    plan = {
        (1, 2): "1y1 1x1",
        (1, 3): "2y1 2x1",
        (2, 1): "0y1 0x1",
        (2, 3): "1y2 1x2",
        (3, 0): "2y2 1x3",
        (3, 1): "1x4 1y3",
        (3, 2): "2x2 0y2",
        (3, 3): "0x2 2x3",
        (4, 0): "1x5 2y3",
        (4, 1): "2x4 1y4",
        (4, 2): "0x3",
        (4, 3): "2x5",
        (5, 0): "0x4 0x5 0y3",
        (5, 1): "2y4",
        (6, 0): "0y4 1y5",
        (6, 3): "2y5",
        (7, 0): "0y5",
    }
    for d in range(1, 8):
        for p in range(4):
            take_t(d, p)
            for word in plan.get((d, p), "").split():
                w[int(word[0])][word[1:]]()
            if (d, p) == (5, 2):
                spread_spectrum()
    for load in own_tokens:
        load.wait()
    w[1]["finish"]()
    w[2]["finish"]()

    def project(origin, which, fresh=False):
        block = tbuf[origin].reshape(256, 256)
        rows = pl.ds(pl.multiple_of(origin * 256, 256), 256)
        for j in which:
            part = jnp.dot(block, wbuf[j, rows, :], preferred_element_type=F32)
            acc[j] = part if fresh else acc[j] + part

    def project_near(which):
        project(z, which, True)
        for d in range(1, 8):
            project((z + 16 - d) % 16, which)
            project((z + d) % 16, which)

    project_near((1, 2))
    for p in range(4):
        take_t(8, p)
    project((z + 8) % 16, (1, 2))

    by_m0 = table[:, 1536:1792]
    for half in range(2):
        lanes = slice(128 * half, 128 * half + 128)
        gated = (acc[1, :, lanes] * acc[2, :, lanes]).astype(BF16)
        gated = jnp.dot(by_m0, gated, preferred_element_type=F32)
        groups = swap_blocks([gated[16 * i : 16 * i + 16, :] for i in range(16)])
        for i in range(16):
            gbuf[half, i] = groups[i].astype(BF16)
        spread(lambda peer: gbuf.at[half, peer], xbuf.at[half, s], 1 + half)
        xbuf[half, s] = gbuf[half, s]

    o["start"]()
    w[0]["finish"]()
    project_near((0,))
    project((z + 8) % 16, (0,))
    collect(sbuf.at[:, pl.ds(0, 240)], 0)

    cos, sin = twist[0][:, None, :], twist[1][:, None, :]
    first, mix, unmix = table[:, :1024], table[:, 1024:1280], table[:, 1280:1536]
    for half in range(2):
        collect(xbuf.at[half, pl.ds(0, 15)], 1 + half)
        signal = xbuf[half].reshape(256, 128).astype(F32).T.astype(BF16)
        a = jnp.dot(signal, first, preferred_element_type=F32)
        a_re, a_im = a[:, :512].reshape(16, 8, 512), a[:, 512:].reshape(16, 8, 512)
        b_re = (a_re * cos + a_im * sin).reshape(128, 512)
        b_im = (a_im * cos - a_re * sin).reshape(128, 512)
        b = jnp.concatenate([b_re, b_im], axis=0).astype(BF16)
        u = jnp.dot(mix, b, preferred_element_type=F32)
        u_re, u_im = u[:128], u[128:]
        f_re, f_im = (
            sbuf[part].astype(F32).reshape(16, 2, 8, 512)[:, half].reshape(128, 512) for part in range(2)
        )
        v = jnp.concatenate([u_re * f_re - u_im * f_im, u_re * f_im + u_im * f_re], axis=0).astype(BF16)
        c = jnp.dot(unmix, v, preferred_element_type=F32)
        c_re, c_im = c[:128].reshape(16, 8, 512), c[128:].reshape(16, 8, 512)
        d_re = (c_re * cos - c_im * sin).reshape(128, 512)
        d_im = (c_im * cos + c_re * sin).reshape(128, 512)
        d_all = jnp.concatenate([d_re, d_im], axis=1).astype(BF16)
        y = lax.dot_general(first, d_all, (((1,), (1,)), ((), ())), preferred_element_type=F32)
        ybuf[half] = (y * (1.0 / 8192.0)).astype(BF16).reshape(16, 16, 128)
        spread(lambda peer: ybuf.at[half, peer], rbuf.at[half, s], 3 + half)
        rbuf[half, s] = ybuf[half, s]
    o["y1"]()
    o["x1"]()
    o["y2"]()

    for half in range(2):
        collect(rbuf.at[half, pl.ds(0, 15)], 3 + half)
        groups = swap_blocks([rbuf[half, i].astype(F32) for i in range(16)])
        conv = jnp.concatenate(groups, axis=0).astype(BF16)
        conv = jnp.dot(by_m0, conv, preferred_element_type=F32)
        mixed = (acc[0, :, 128 * half : 128 * half + 128] * conv).astype(BF16)
        mbuf[z, 2 * half] = mixed[:128]
        mbuf[z, 2 * half + 1] = mixed[128:]
        start_m((2 * half, 2 * half + 1))

    total[...] = jnp.zeros_like(total)

    def combine(origin):
        rows = pl.ds(pl.multiple_of(origin * 256, 256), 256)
        halves = [jnp.concatenate([mbuf[origin, 2 * half], mbuf[origin, 2 * half + 1]], axis=0) for half in range(2)]
        block = jnp.concatenate(halves, axis=1)
        total[...] += jnp.dot(block, obuf[rows, :], preferred_element_type=F32)

    plan = {
        (1, 0): "x2 x3",
        (1, 2): "y3 y4 x4",
        (2, 1): "x5",
        (3, 0): "y5",
        (4, 0): "finish",
    }
    ready = [[], [], [], [], [0, 1, 2], [3, 4], [5, 6], [7], [8]]
    for d in range(1, 9):
        for p in range(4):
            take_m(d, p)
            for word in plan.get((d, p), "").split():
                o[word]()
        for near in ready[d]:
            combine((z + 16 - near) % 16)
            if 0 < near < 8:
                combine((z + near) % 16)
    out[...] = total[...].astype(BF16)

    for copy in sends:
        copy.wait_send()
    for each in w + [o]:
        each["drain"]()
    drain_many(sbuf.at[:, pl.ds(0, 240)], 0)
    for half in range(2):
        drain_many(xbuf.at[half, pl.ds(0, 15)], 1 + half)
        drain_many(rbuf.at[half, pl.ds(0, 15)], 3 + half)


def body(tokens, in_weights, out_weights, spectrum):
    dma = pltpu.SemaphoreType.DMA
    any_spec = pl.BlockSpec(memory_space=pl.ANY)
    return pl.pallas_call(
        kernel,
        out_shape=jax.ShapeDtypeStruct((256, 256), BF16),
        in_specs=[any_spec] * 6,
        out_specs=pl.BlockSpec(memory_space=pltpu.VMEM),
        scratch_shapes=[
            pltpu.VMEM((16, 4, 64, 256), BF16),
            pltpu.VMEM((3, 4096, 256), BF16),
            pltpu.VMEM((4096, 256), BF16),
            pltpu.VMEM((16, 4, 128, 128), BF16),
            pltpu.VMEM((2, 256, 512), F32),
            pltpu.VMEM((2, 256, 512), BF16),
            pltpu.VMEM((2, 256, 512), BF16),
            pltpu.VMEM((2, 16, 16, 128), BF16),
            pltpu.VMEM((2, 16, 16, 128), BF16),
            pltpu.VMEM((2, 16, 16, 128), BF16),
            pltpu.VMEM((2, 16, 16, 128), BF16),
            pltpu.VMEM((3, 256, 256), F32),
            pltpu.VMEM((256, 256), F32),
            pltpu.VMEM((256, 2048), BF16),
            pltpu.VMEM((2, 16, 512), F32),
            dma((2, 8, 4)),
            dma((2, 8, 4)),
            dma((2, 8, 4)),
            dma((2, 8, 4)),
            dma((4, 14)),
            dma((4, 14)),
            dma((4,)),
            dma((4,)),
            dma((5,)),
            dma((5,)),
            dma((11,)),
        ],
        compiler_params=pltpu.CompilerParams(
            collective_id=0, has_side_effects=True, vmem_limit_bytes=60 * 1024 * 1024
        ),
    )(tokens, in_weights, out_weights, spectrum, *tables())


def solution(mesh):
    placed = (
        P(("batch", "seq"), "chan"),
        P(None, "seq", "chan"),
        P("seq", "chan"),
        P(None, "chan", "seq"),
    )
    return jax.shard_map(
        body, mesh=mesh, in_specs=placed, out_specs=P(("batch", "seq"), "chan"), check_vma=False
    )
```
